256 devices in a mesh: tm: 16 (over x_hi, y, core), chan: 16 (over z, x_lo).
Axes of the slice: x: 4 (x_hi: 2, x_lo: 2; x = x_hi * 2 + x_lo), y: 4, z: 8, core: 2. Of those that a mesh axis runs over, the one named last changes fastest.
Arguments:
- voltages: bfloat16 [2, 512, 524288], P(None, 'chan', 'tm'), may hold values from -6 to 6
- filter_taps: float32 [16, 1024], replicated, may hold values from -1.5 to 1.5
- slot_station: int32 [256], replicated, may hold values from 0 to 255, each once
- pair_blocks: int32 [10, 2], replicated, may hold values from 0 to 3, as said below
Outputs:
- visibilities: float32 [1024, 10, 2, 128, 128], P(('chan', 'tm'))
The draws below stay inside these ranges and needn't reach their ends.
Inputs may be any that keep to these rules, and one draw needn't show every extreme that they name: `slot_station`: each station stands in exactly one slot. `pair_blocks`: every pair (row tile, column tile) of tiles of 128 inputs with row tile >= column tile stands in exactly one row, row tile first.
All inputs are finite; a program needn't handle non-finite values.
Results may differ from the reference program's by a relative error of at most 0.0041.
Values may be sent and summed in bfloat16 or wider, within the bound.
No kernel may reach another device: no remote copies, remote signals or barrier semaphores. Data moves between devices by JAX's collectives and lax.ppermute only.
A program may use at most 192 MiB of HBM per device.

```python
import math
import jax
import jax.numpy as jnp
import numpy as np
from jax import lax

STATIONS = 256
NCH = 1024
TAPS = 16
TILE = 128
INPUTS = 512
SPECTRA = 512
SAMPLES = 524288
NT = 4
NB = 10


def draw_pair_blocks(key, part):
    key = jax.random.fold_in(key, 7)
    listing = []
    for row_tile in range(NT):
        for col_tile in range(row_tile + 1):
            listing.append([row_tile, col_tile])
    pair_table = jnp.asarray(np.array(listing, dtype=np.int32))
    shuffle = jax.random.permutation(key, NB)
    return pair_table[shuffle].astype(jnp.int32)


def block_levels(rng, extent, pieces, low, high):
    def one(axis_at, shards_of):
        heights = jax.random.uniform(jax.random.fold_in(jax.random.fold_in(rng, 6), axis_at), (shards_of,), jnp.float32, low / len(pieces), high / len(pieces))
        return jnp.repeat(jnp.exp(heights), extent[axis_at] // shards_of).reshape((-1,) + (1,) * (len(extent) - axis_at - 1))

    factor_of = one(*pieces[0])
    for cut in pieces[1:]:
        factor_of = factor_of * one(*cut)
    return factor_of


def centred(stream_key, dims, spread, reach, split=(), kind=jnp.bfloat16):
    result = jax.random.normal(stream_key, dims, jnp.float32) * spread
    if len(split) > 0:
        result = block_levels(stream_key, dims, split, -0.22, 0.18) * result
    return jnp.clip(result, min=-reach, max=reach).astype(kind)


def setup_inputs(seed: int = 0) -> dict:
    seeds = jax.random.split(jax.random.key(seed), 5)
    return {
        "voltages": centred(seeds[0], (2, INPUTS, SAMPLES), 1.0, 6.0, ((1, 16), (2, 16))),
        "filter_taps": centred(seeds[1], (TAPS, NCH), 0.25, 1.5, (), jnp.float32),
        "slot_station": jax.random.permutation(seeds[2], STATIONS).astype(jnp.int32),
        "pair_blocks": draw_pair_blocks(jax.random.fold_in(seeds[4], 71), 0),
    }


def dft_table(channels):
    indices = jnp.arange(channels, dtype=jnp.int32)
    products = indices[:, None] * indices[None, :] % channels
    angles = products.astype(jnp.float32) * (2.0 * math.pi / channels)
    cosine = jnp.cos(angles) / math.sqrt(channels)
    sine_part = jnp.sin(angles) / math.sqrt(channels)
    upper_half = jnp.concatenate([cosine, -sine_part], 1)
    lower_half = jnp.concatenate([sine_part, cosine], 1)
    return jnp.concatenate([upper_half, lower_half], 0).astype(jnp.bfloat16)

def slot_order(slot_station, inputs):
    stations = slot_station.shape[0]
    positions = jnp.arange(stations, dtype=jnp.int32)
    inverse = jnp.zeros((stations,), jnp.int32).at[slot_station].set(positions)
    indices = jnp.arange(inputs, dtype=jnp.int32)
    return 2 * inverse[indices // 2] + indices % 2

def channelize(group_block, filter_taps, table):
    group_size = group_block.shape[1]
    leading = jnp.zeros((2, group_size, (TAPS - 1) * NCH), jnp.bfloat16)
    extended = jnp.concatenate([leading, group_block], 2).reshape(2, group_size, SPECTRA + TAPS - 1, NCH)
    summed = jnp.zeros((2, group_size, SPECTRA, NCH), jnp.float32)
    for tap_index in range(TAPS):
        summed = summed + filter_taps[tap_index] * extended[:, :, tap_index:tap_index + SPECTRA, :].astype(jnp.float32)
    filtered = summed.astype(jnp.bfloat16)
    joined = jnp.concatenate([filtered[0], filtered[1]], -1)
    spectra = jnp.einsum('ifn,nk->kfi', joined.astype(jnp.float32), table.astype(jnp.float32))
    return spectra.astype(jnp.bfloat16)

def combine_parts(gram_part, tile_size):
    real_part = gram_part[:tile_size, :tile_size] + gram_part[tile_size:, tile_size:]
    imag_part = gram_part[tile_size:, :tile_size] - gram_part[:tile_size, tile_size:]
    return jnp.stack([real_part, imag_part])

def correlate(channel_data, pair_blocks):

    def one_block(pair):
        row_cols = lax.dynamic_slice_in_dim(channel_data, pair[0] * TILE, TILE, 2)
        col_cols = lax.dynamic_slice_in_dim(channel_data, pair[1] * TILE, TILE, 2)
        left_cols = jnp.concatenate([row_cols[0], row_cols[1]], 1)
        right_cols = jnp.concatenate([col_cols[0], col_cols[1]], 1)
        gram_part = jnp.dot(left_cols.T, right_cols, preferred_element_type=jnp.float32)
        return combine_parts(gram_part, TILE) * (1.0 / SPECTRA)
    return jax.vmap(one_block)(pair_blocks)

def reference(voltages, filter_taps, slot_station, pair_blocks):
    input_slot = slot_order(slot_station, INPUTS)
    ordered = voltages[:, input_slot, :]
    group_count = 16
    group_size = INPUTS // group_count
    groups = jnp.moveaxis(ordered.reshape(2, group_count, group_size, SAMPLES), 1, 0)
    table = dft_table(NCH)
    spectra = lax.map(lambda group_block: channelize(group_block, filter_taps, table), groups)
    spectra = jnp.moveaxis(spectra, 0, 2).reshape(2, NCH, SPECTRA, INPUTS)
    per_channel = jnp.moveaxis(spectra, 1, 0)
    return lax.map(lambda channel_data: correlate(channel_data, pair_blocks), per_channel)
```

```python
import functools
import math

import jax
import jax.numpy as jnp
import numpy as np
from jax import lax
from jax.experimental import pallas as pl
from jax.experimental.pallas import tpu as pltpu
from jax.sharding import PartitionSpec as P

TILE = 128
OWNERS = ("chan", "tm")
NT = (((1,), (1,)), ((), ()))


def dft_rows(channels, per_owner):
    index = np.arange(channels, dtype=np.int32)
    angles = (index[:, None] * index[None, :] % channels).astype(np.float32)
    angles = angles * np.float32(2.0 * math.pi / channels)
    cosine = np.cos(angles) / np.float32(math.sqrt(channels))
    sine = np.sin(angles) / np.float32(math.sqrt(channels))
    real = np.concatenate([cosine, sine], 1)
    imag = np.concatenate([-sine, cosine], 1)
    return np.stack([real, imag], 1).reshape(2 * channels, 2 * channels).astype(jnp.bfloat16)


def front_kernel(
    first, frames, inputs, channels, sources, *refs
):
    n_in = 1 + max(s[0] for s in sources)
    hbm = refs[:n_in]
    taps_ref, table_hbm, out_ref = refs[n_in : n_in + 3]
    bufs = refs[n_in + 3 : 2 * n_in + 3]
    table_ref, joined, sems, table_sem = refs[2 * n_in + 3 :]
    tap_count = taps_ref.shape[0]
    half = 16
    groups = [(q, h) for q in range(2) for h in range(inputs // half)]
    spans = []
    for operand in range(n_in):
        used = [s[1] for s in sources if s[0] == operand]
        spans.append((min(used), max(used) + 1))

    def copies(at):
        q, h = groups[at]
        rows = pl.ds(h * half, half)
        return [
            pltpu.make_async_copy(
                hbm[p].at[q, rows, pl.ds(spans[p][0] * channels, (spans[p][1] - spans[p][0]) * channels)],
                bufs[p].at[q, rows],
                sems.at[p, at],
            )
            for p in range(n_in)
        ]

    for at in range(len(groups)):
        for copy in copies(at):
            copy.start()
    table_copy = pltpu.make_async_copy(table_hbm, table_ref, table_sem)
    table_copy.start()
    for at, (q, h) in enumerate(groups):
        for copy in copies(at):
            copy.wait()

        def columns(step, carry, q=q, h=h):
            lane = pl.multiple_of(step * 128, 128)
            taps = [taps_ref[pl.ds(t, 1), pl.ds(lane, 128)] for t in range(tap_count)]
            window = []
            for operand, frame in sources:
                place = pl.multiple_of((frame - spans[operand][0]) * channels + lane, 128)
                window.append(
                    bufs[operand][q, pl.ds(h * half, half), pl.ds(place, 128)].astype(jnp.float32)
                )
            for s in range(frames):
                total = window[s] * taps[0]
                for t in range(1, tap_count):
                    total = total + window[s + t] * taps[t]
                joined[pl.ds(s * inputs + h * half, half), pl.ds(pl.multiple_of(q * channels + lane, 128), 128)] = (
                    total.astype(jnp.bfloat16)
                )
            return carry

        lax.fori_loop(0, channels // 128, columns, 0)
    table_copy.wait()
    rows = 256

    def transform(step, carry):
        at = pl.ds(pl.multiple_of(step * rows, rows), rows)
        out_ref[at, :] = lax.dot_general(
            table_ref[at, :], joined[...], NT, preferred_element_type=jnp.float32
        ).astype(jnp.bfloat16)
        return carry

    lax.fori_loop(0, out_ref.shape[0] // rows, transform, 0)


def front(operands, taps, table, sources, frames):
    inputs = operands[0].shape[1]
    channels = taps.shape[1]
    n_in = len(operands)
    spans = []
    for operand in range(n_in):
        used = [s[1] for s in sources if s[0] == operand]
        spans.append(max(used) + 1 - min(used))
    size = 2 * channels
    return pl.pallas_call(
        functools.partial(front_kernel, 0, frames, inputs, channels, sources),
        out_shape=jax.ShapeDtypeStruct((size, frames * inputs), jnp.bfloat16),
        in_specs=[pl.BlockSpec(memory_space=pl.ANY)] * n_in
        + [pl.BlockSpec(memory_space=pltpu.VMEM), pl.BlockSpec(memory_space=pl.ANY)],
        out_specs=pl.BlockSpec(memory_space=pltpu.VMEM),
        scratch_shapes=[pltpu.VMEM((2, inputs, span * channels), jnp.bfloat16) for span in spans]
        + [
            pltpu.VMEM(table.shape, jnp.bfloat16),
            pltpu.VMEM((frames * inputs, size), jnp.bfloat16),
            pltpu.SemaphoreType.DMA((n_in, 2 * (inputs // 16))),
            pltpu.SemaphoreType.DMA,
        ],
        compiler_params=pltpu.CompilerParams(vmem_limit_bytes=40 * 2**20),
        cost_estimate=pl.CostEstimate(
            flops=2 * size * size * frames * inputs + 64 * frames * inputs * size,
            bytes_accessed=16 * 2**20,
            transcendentals=0,
        ),
        name="front",
    )(*operands, taps, table)


def sort_rows(times, parts):
    size = times * parts
    matrix = np.zeros((size, size), np.float32)
    for part in range(parts):
        for time in range(times):
            matrix[part * times + time, time * parts + part] = 1
    return matrix.astype(jnp.bfloat16)


def sort_lanes(group, block):
    size = group * group * block
    index = np.arange(size).reshape(group, group, block)
    matrix = np.zeros((size, size), np.float32)
    matrix[index.transpose(1, 0, 2).reshape(-1), np.arange(size)] = 1
    return matrix.astype(jnp.bfloat16)


def dot(left, right):
    return jnp.dot(left, right, preferred_element_type=jnp.float32).astype(jnp.bfloat16)


def gather_kernel(n_chan, n_time, parts, inputs, frames, got, rows_ref, lanes_ref, place_ref, out, sorted_rows, ordered):
    block = n_time * parts
    group = 128 // inputs
    for c in range(n_chan):
        at = pl.ds(c * block, block)
        sorted_rows[at, :] = dot(rows_ref[...], got[at, :])
    for a in range(n_chan // group):
        for g in range(frames // group):
            side = jnp.concatenate(
                [
                    sorted_rows[pl.ds((a * group + b) * block, block), pl.ds(g * 128, 128)]
                    for b in range(group)
                ],
                1,
            )
            turned = dot(side, lanes_ref[...])
            for j in range(group):
                for part in range(parts):
                    ordered[part, pl.ds((g * group + j) * n_time, n_time), pl.ds(a * 128, 128)] = turned[
                        part * n_time : (part + 1) * n_time, j * 128 : (j + 1) * 128
                    ]
    for part in range(parts):
        out[part] = lax.dot_general(
            place_ref[...], ordered[part], NT, preferred_element_type=jnp.float32
        ).astype(jnp.bfloat16)


def gather(got, rows, lanes, place, n_chan, n_time, parts, inputs):
    frames = got.shape[1] // inputs
    total = n_chan * inputs
    return pl.pallas_call(
        functools.partial(gather_kernel, n_chan, n_time, parts, inputs, frames),
        out_shape=jax.ShapeDtypeStruct((parts, total, n_time * frames), jnp.bfloat16),
        in_specs=[pl.BlockSpec(memory_space=pltpu.VMEM)] * 4,
        out_specs=pl.BlockSpec(memory_space=pltpu.VMEM),
        scratch_shapes=[
            pltpu.VMEM(got.shape, jnp.bfloat16),
            pltpu.VMEM((parts, n_time * frames, total), jnp.bfloat16),
        ],
        compiler_params=pltpu.CompilerParams(vmem_limit_bytes=32 * 2**20),
        cost_estimate=pl.CostEstimate(flops=4 * 10**9, bytes_accessed=8 * 2**20, transcendentals=0),
        name="gather",
    )(got, rows, lanes, place)


def correlate_kernel(scale, pairs, *refs):
    pieces, out = refs[:-1], refs[-1]
    for b in range(out.shape[1]):
        sides = []
        for end in range(2):
            at = pl.ds(pl.multiple_of(pairs[b, end] * TILE, TILE), TILE)
            sides.append([jnp.concatenate([piece[0, at, :], piece[1, at, :]], 0) for piece in pieces])
        gram = sum(
            lax.dot_general(left, right, NT, preferred_element_type=jnp.float32)
            for left, right in zip(*sides)
        )
        out[0, b, 0] = (gram[:TILE, :TILE] + gram[TILE:, TILE:]) * scale
        out[0, b, 1] = (gram[TILE:, :TILE] - gram[:TILE, TILE:]) * scale


def correlate(pieces, pair_blocks, scale):
    parts, inputs, times = pieces[0].shape
    blocks = pair_blocks.shape[0]
    return pl.pallas_call(
        functools.partial(correlate_kernel, scale),
        out_shape=jax.ShapeDtypeStruct((parts // 2, blocks, 2, TILE, TILE), jnp.float32),
        grid_spec=pltpu.PrefetchScalarGridSpec(
            num_scalar_prefetch=1,
            grid=(parts // 2,),
            in_specs=[pl.BlockSpec((2, inputs, times), lambda k, pairs: (k, 0, 0))] * len(pieces),
            out_specs=pl.BlockSpec((1, blocks, 2, TILE, TILE), lambda k, pairs: (k, 0, 0, 0, 0)),
        ),
        compiler_params=pltpu.CompilerParams(vmem_limit_bytes=32 * 2**20),
        name="correlate",
    )(pair_blocks, *pieces)


def local(voltages, filter_taps, slot_station, pair_blocks):
    tap_count, channels = filter_taps.shape
    inputs = voltages.shape[1]
    frame_count = voltages.shape[2] // channels
    n_chan = lax.axis_size("chan")
    n_time = lax.axis_size("tm")
    owners = n_chan * n_time
    per_owner = channels // owners
    parts = 2 * per_owner
    history = tap_count - 1
    tail = voltages[:, :, voltages.shape[2] - history * channels :]
    earlier = lax.ppermute(tail, "tm", [(i, i + 1) for i in range(n_time - 1)])
    table = jnp.asarray(dft_rows(channels, per_owner))
    cut = frame_count // 2

    def turn(spectra):
        pieces = spectra.reshape(owners, parts, -1)
        return lax.all_to_all(pieces, OWNERS, split_axis=0, concat_axis=0, tiled=True).reshape(owners * parts, -1)

    late = [(0, f) for f in range(cut - history, frame_count)]
    early = [(0, f) for f in range(history)] + [(1, f) for f in range(cut)]
    got_late = turn(front([voltages], filter_taps, table, late, frame_count - cut))
    got_early = turn(front([earlier, voltages], filter_taps, table, early, cut))

    total = n_chan * inputs
    index = jnp.arange(total, dtype=jnp.int32)
    station_in = jnp.repeat(slot_station, 2)
    place = (station_in[None, :] == index[:, None] // 2) & (index[None, :] % 2 == index[:, None] % 2)
    place = place.astype(jnp.bfloat16)
    rows = jnp.asarray(sort_rows(n_time, parts))
    lanes = jnp.asarray(sort_lanes(128 // inputs, inputs))
    pieces = [gather(got, rows, lanes, place, n_chan, n_time, parts, inputs) for got in (got_late, got_early)]
    return correlate(pieces, pair_blocks, 1.0 / (n_time * frame_count))


def solution(mesh):
    in_specs = (P(None, "chan", "tm"), P(), P(), P())
    out_specs = P(("chan", "tm"), None, None, None, None)
    return jax.shard_map(local, mesh=mesh, in_specs=in_specs, out_specs=out_specs, check_vma=False)
```

```python
import functools
import math

import jax
import jax.numpy as jnp
import numpy as np
from jax import lax
from jax.experimental import pallas as pl
from jax.experimental.pallas import tpu as pltpu
from jax.sharding import PartitionSpec as P

TILE = 128
OWNERS = ("chan", "tm")
NT = (((1,), (1,)), ((), ()))


def dft_rows(channels, per_owner):
    index = np.arange(channels, dtype=np.int32)
    angles = (index[:, None] * index[None, :] % channels).astype(np.float32)
    angles = angles * np.float32(2.0 * math.pi / channels)
    cosine = np.cos(angles) / np.float32(math.sqrt(channels))
    sine = np.sin(angles) / np.float32(math.sqrt(channels))
    real = np.concatenate([cosine, sine], 1)
    imag = np.concatenate([-sine, cosine], 1)
    return np.stack([real, imag], 1).reshape(2 * channels, 2 * channels).astype(jnp.bfloat16)


STRIP = 8


def strips(segments, n_in):
    cuts, bounds = [], []
    for operand in range(n_in):
        used = [at for window in segments for where, at in window if where == operand]
        first, last = min(used), max(used) + 1
        bounds.append((first, last - first))
        for start in range(first, last, STRIP):
            cuts.append((operand, start, min(STRIP, last - start)))
    return cuts, bounds


def front_kernel(inputs, channels, segments, masked, n_in, *refs):
    keep_ref, hbm = refs[0], refs[1 : 1 + n_in]
    taps_ref, table_hbm, out_hbm = refs[1 + n_in : 4 + n_in]
    bufs = refs[4 + n_in : 4 + 2 * n_in]
    table_ref, joined, out, sems, table_sems, out_sems = refs[4 + 2 * n_in :]
    tap_count = taps_ref.shape[0]
    half = 16
    groups = [(q, h) for q in range(2) for h in range(inputs // half)]
    cuts, bounds = strips(segments, n_in)

    def copies(at):
        q, h = groups[at]
        rows = pl.ds(h * half, half)
        return [
            pltpu.make_async_copy(
                hbm[p].at[q, rows, pl.ds(first * channels, count * channels)],
                bufs[p].at[q, rows, pl.ds((first - bounds[p][0]) * channels, count * channels)],
                sems.at[at, i],
            )
            for i, (p, first, count) in enumerate(cuts)
        ]

    size = table_ref.shape[0]
    tile = size // table_sems.shape[0]

    def table_copy(i):
        at = pl.ds(i * tile, tile)
        return pltpu.make_async_copy(table_hbm.at[at], table_ref.at[at], table_sems.at[i])

    def filtered(q, h, step):
        lane = pl.multiple_of(step * 128, 128)
        rows = pl.ds(h * half, half)
        taps = [taps_ref[pl.ds(t, 1), pl.ds(lane, 128)] for t in range(tap_count)]
        base = 0
        for number, window in enumerate(segments):
            count = len(window) - tap_count + 1
            totals = [None] * count
            for at, (operand, frame) in enumerate(window):
                place = pl.multiple_of((frame - bounds[operand][0]) * channels + lane, 128)
                value = bufs[operand][q, rows, pl.ds(place, 128)].astype(jnp.float32)
                if number == masked and at < tap_count - 1:
                    value = value * keep_ref[0]
                for s in range(max(0, at - tap_count + 1), min(count, at + 1)):
                    term = value * taps[at - s]
                    totals[s] = term if totals[s] is None else totals[s] + term
                s = at - tap_count + 1
                if s >= 0:
                    joined[
                        pl.ds((base + s) * inputs + h * half, half),
                        pl.ds(pl.multiple_of(q * channels + lane, 128), 128),
                    ] = totals[s].astype(jnp.bfloat16)
            base += count

    for at in range(len(groups)):
        for copy in copies(at):
            copy.start()
    for at, (q, h) in enumerate(groups):
        for copy in copies(at):
            copy.wait()
        if at == 0:
            for i in range(table_sems.shape[0]):
                table_copy(i).start()

        def columns(step, carry, q=q, h=h):
            filtered(q, h, step)
            return carry

        lax.fori_loop(0, channels // 128, columns, 0)
    large = size // out_sems.shape[0]
    sent = []
    for i in range(out_sems.shape[0]):
        rows = pl.ds(i * large, large)
        for j in range(i * large // tile, (i + 1) * large // tile):
            table_copy(j).wait()
        out[rows, :] = lax.dot_general(
            table_ref[rows, :], joined[...], NT, preferred_element_type=jnp.float32
        ).astype(jnp.bfloat16)
        sent.append(pltpu.make_async_copy(out.at[rows], out_hbm.at[rows], out_sems.at[i]))
        sent[-1].start()
    for copy in sent:
        copy.wait()


def front(keep, operands, taps, table, segments, masked):
    inputs = operands[0].shape[1]
    channels = taps.shape[1]
    n_in = len(operands)
    cuts, bounds = strips(segments, n_in)
    size = 2 * channels
    lanes = inputs * sum(len(window) - taps.shape[0] + 1 for window in segments)
    return pl.pallas_call(
        functools.partial(front_kernel, inputs, channels, segments, masked, n_in),
        out_shape=jax.ShapeDtypeStruct((size, lanes), jnp.bfloat16),
        in_specs=[pl.BlockSpec(memory_space=pltpu.SMEM)]
        + [pl.BlockSpec(memory_space=pl.ANY)] * n_in
        + [pl.BlockSpec(memory_space=pltpu.VMEM), pl.BlockSpec(memory_space=pl.ANY)],
        out_specs=pl.BlockSpec(memory_space=pl.ANY),
        scratch_shapes=[pltpu.VMEM((2, inputs, span * channels), jnp.bfloat16) for _, span in bounds]
        + [
            pltpu.VMEM(table.shape, jnp.bfloat16),
            pltpu.VMEM((lanes, size), jnp.bfloat16),
            pltpu.VMEM((size, lanes), jnp.bfloat16),
            pltpu.SemaphoreType.DMA((2 * (inputs // 16), len(cuts))),
            pltpu.SemaphoreType.DMA((8,)),
            pltpu.SemaphoreType.DMA((4,)),
        ],
        compiler_params=pltpu.CompilerParams(vmem_limit_bytes=56 * 2**20),
        cost_estimate=pl.CostEstimate(
            flops=2 * size * size * lanes, bytes_accessed=16 * 2**20, transcendentals=0
        ),
        name="front",
    )(keep, *operands, taps, table)


def sort_rows(times, parts):
    size = times * parts
    matrix = np.zeros((size, size), np.float32)
    for part in range(parts):
        for time in range(times):
            matrix[part * times + time, time * parts + part] = 1
    return matrix.astype(jnp.bfloat16)


def sort_lanes(group, block):
    size = group * group * block
    index = np.arange(size).reshape(group, group, block)
    matrix = np.zeros((size, size), np.float32)
    matrix[index.transpose(1, 0, 2).reshape(-1), np.arange(size)] = 1
    return matrix.astype(jnp.bfloat16)


def dot(left, right):
    return jnp.dot(left, right, preferred_element_type=jnp.float32).astype(jnp.bfloat16)


def gather_kernel(n_chan, n_time, parts, inputs, frames, got, rows_ref, lanes_ref, place_ref, out, sorted_rows, ordered):
    block = n_time * parts
    group = 128 // inputs
    for c in range(n_chan):
        at = pl.ds(c * block, block)
        sorted_rows[at, :] = dot(rows_ref[...], got[at, :])
    for a in range(n_chan // group):
        for g in range(frames // group):
            side = jnp.concatenate(
                [
                    sorted_rows[pl.ds((a * group + b) * block, block), pl.ds(g * 128, 128)]
                    for b in range(group)
                ],
                1,
            )
            turned = dot(side, lanes_ref[...])
            for j in range(group):
                for part in range(parts):
                    ordered[part, pl.ds((g * group + j) * n_time, n_time), pl.ds(a * 128, 128)] = turned[
                        part * n_time : (part + 1) * n_time, j * 128 : (j + 1) * 128
                    ]
    for part in range(parts):
        out[part] = lax.dot_general(
            place_ref[...], ordered[part], NT, preferred_element_type=jnp.float32
        ).astype(jnp.bfloat16)


def gather(got, rows, lanes, place, n_chan, n_time, parts, inputs):
    frames = got.shape[1] // inputs
    total = n_chan * inputs
    return pl.pallas_call(
        functools.partial(gather_kernel, n_chan, n_time, parts, inputs, frames),
        out_shape=jax.ShapeDtypeStruct((parts, total, n_time * frames), jnp.bfloat16),
        in_specs=[pl.BlockSpec(memory_space=pltpu.VMEM)] * 4,
        out_specs=pl.BlockSpec(memory_space=pltpu.VMEM),
        scratch_shapes=[
            pltpu.VMEM(got.shape, jnp.bfloat16),
            pltpu.VMEM((parts, n_time * frames, total), jnp.bfloat16),
        ],
        compiler_params=pltpu.CompilerParams(vmem_limit_bytes=32 * 2**20),
        cost_estimate=pl.CostEstimate(flops=4 * 10**9, bytes_accessed=8 * 2**20, transcendentals=0),
        name="gather",
    )(got, rows, lanes, place)


def correlate_kernel(scale, pairs, *refs):
    pieces, out = refs[:-1], refs[-1]
    for b in range(out.shape[1]):
        sides = []
        for end in range(2):
            at = pl.ds(pl.multiple_of(pairs[b, end] * TILE, TILE), TILE)
            sides.append([jnp.concatenate([piece[0, at, :], piece[1, at, :]], 0) for piece in pieces])
        gram = sum(
            lax.dot_general(left, right, NT, preferred_element_type=jnp.float32)
            for left, right in zip(*sides)
        )
        out[0, b, 0] = (gram[:TILE, :TILE] + gram[TILE:, TILE:]) * scale
        out[0, b, 1] = (gram[TILE:, :TILE] - gram[:TILE, TILE:]) * scale


def correlate(pieces, pair_blocks, scale):
    parts, inputs, times = pieces[0].shape
    blocks = pair_blocks.shape[0]
    return pl.pallas_call(
        functools.partial(correlate_kernel, scale),
        out_shape=jax.ShapeDtypeStruct((parts // 2, blocks, 2, TILE, TILE), jnp.float32),
        grid_spec=pltpu.PrefetchScalarGridSpec(
            num_scalar_prefetch=1,
            grid=(parts // 2,),
            in_specs=[pl.BlockSpec((2, inputs, times), lambda k, pairs: (k, 0, 0))] * len(pieces),
            out_specs=pl.BlockSpec((1, blocks, 2, TILE, TILE), lambda k, pairs: (k, 0, 0, 0, 0)),
        ),
        compiler_params=pltpu.CompilerParams(vmem_limit_bytes=32 * 2**20),
        name="correlate",
    )(pair_blocks, *pieces)


def local(voltages, filter_taps, slot_station, pair_blocks):
    tap_count, channels = filter_taps.shape
    inputs = voltages.shape[1]
    frame_count = voltages.shape[2] // channels
    n_chan = lax.axis_size("chan")
    n_time = lax.axis_size("tm")
    owners = n_chan * n_time
    per_owner = channels // owners
    parts = 2 * per_owner
    history = tap_count - 1
    ahead = history // 2
    cut = frame_count // 2
    table = jnp.asarray(dft_rows(channels, per_owner))
    t = lax.axis_index("tm")
    keep = (t < n_time - 1).astype(jnp.float32).reshape(1)

    def turn(spectra):
        pieces = spectra.reshape(owners, parts, -1)
        return lax.all_to_all(pieces, OWNERS, split_axis=0, concat_axis=0, tiled=True).reshape(owners * parts, -1)

    late = [[(0, f) for f in range(cut - history, frame_count)]]
    sent_late = front(keep, [voltages], filter_taps, table, late, None)
    got_late = turn(sent_late)
    behind = history - ahead
    tail = voltages[:, :, (frame_count - behind) * channels :]
    head = voltages[:, :, : ahead * channels]
    before = lax.ppermute(tail, "tm", [(i, i + 1) for i in range(n_time - 1)])
    after = lax.ppermute(head, "tm", [(i, (i - 1) % n_time) for i in range(n_time)])
    operands, _ = lax.optimization_barrier(([before, voltages, after], sent_late))
    early = [
        [(0, f) for f in range(behind)] + [(1, f) for f in range(cut)],
        [(1, f) for f in range(frame_count - history, frame_count)] + [(2, f) for f in range(ahead)],
    ]
    got_early = turn(front(keep, operands, filter_taps, table, early, 1))

    total = n_chan * inputs
    index = jnp.arange(total, dtype=jnp.int32)
    station_in = jnp.repeat(slot_station, 2)
    place = (station_in[None, :] == index[:, None] // 2) & (index[None, :] % 2 == index[:, None] % 2)
    place = place.astype(jnp.bfloat16)
    rows = jnp.asarray(sort_rows(n_time, parts))
    lanes = jnp.asarray(sort_lanes(128 // inputs, inputs))
    pieces = [gather(got, rows, lanes, place, n_chan, n_time, parts, inputs) for got in (got_late, got_early)]
    return correlate(pieces, pair_blocks, 1.0 / (n_time * frame_count))


def solution(mesh):
    in_specs = (P(None, "chan", "tm"), P(), P(), P())
    out_specs = P(("chan", "tm"), None, None, None, None)
    return jax.shard_map(local, mesh=mesh, in_specs=in_specs, out_specs=out_specs, check_vma=False)
```

```python
import functools
import math

import jax
import jax.numpy as jnp
import numpy as np
from jax import lax
from jax.experimental import pallas as pl
from jax.experimental.pallas import tpu as pltpu
from jax.sharding import PartitionSpec as P

TILE = 128
OWNERS = ("chan", "tm")
NT = (((1,), (1,)), ((), ()))


def dft_half(channels, per_owner):
    index = np.arange(channels, dtype=np.int32)
    angles = (index[:, None] * index[None, :] % channels).astype(np.float32)
    angles = angles * np.float32(2.0 * math.pi / channels)
    half = channels // 2
    tiles = np.arange(half).reshape(2, -1, per_owner).transpose(1, 0, 2).reshape(-1)
    last = np.zeros(16, np.int32)
    last[0], last[per_owner] = half // 2, half
    picked = np.concatenate([tiles, last])
    tables = [f(angles[picked]) / np.float32(math.sqrt(channels)) for f in (np.cos, np.sin)]
    return np.concatenate(tables, 0).astype(jnp.bfloat16)


STRIP = 8


def strips(segments, n_in):
    cuts, bounds = [], []
    for operand in range(n_in):
        used = [at for window in segments for where, at in window if where == operand]
        first, last = min(used), max(used) + 1
        bounds.append((first, last - first))
        for start in range(first, last, STRIP):
            cuts.append((operand, start, min(STRIP, last - start)))
    return cuts, bounds


def front_kernel(inputs, channels, segments, masked, n_in, *refs):
    keep_ref, hbm = refs[0], refs[1 : 1 + n_in]
    taps_ref, table_hbm, out_hbm = refs[1 + n_in : 4 + n_in]
    bufs = refs[4 + n_in : 4 + 2 * n_in]
    table_ref, joined, out, sems, table_sems, out_sems = refs[4 + 2 * n_in :]
    tap_count = taps_ref.shape[0]
    half = 16
    groups = [(q, h) for q in range(2) for h in range(inputs // half)]
    cuts, bounds = strips(segments, n_in)

    def copies(at):
        q, h = groups[at]
        rows = pl.ds(h * half, half)
        return [
            pltpu.make_async_copy(
                hbm[p].at[q, rows, pl.ds(first * channels, count * channels)],
                bufs[p].at[q, rows, pl.ds((first - bounds[p][0]) * channels, count * channels)],
                sems.at[at, i],
            )
            for i, (p, first, count) in enumerate(cuts)
        ]

    def table_copy(i):
        size = table_ref.shape[0] // table_sems.shape[0]
        at = pl.ds(i * size, size)
        return pltpu.make_async_copy(table_hbm.at[at], table_ref.at[at], table_sems.at[i])

    def filtered(q, h, step):
        lane = pl.multiple_of(step * 128, 128)
        rows = pl.ds(h * half, half)
        taps = [taps_ref[pl.ds(t, 1), pl.ds(lane, 128)] for t in range(tap_count)]
        base = 0
        for number, window in enumerate(segments):
            count = len(window) - tap_count + 1
            totals = [None] * count
            for at, (operand, frame) in enumerate(window):
                place = pl.multiple_of((frame - bounds[operand][0]) * channels + lane, 128)
                value = bufs[operand][q, rows, pl.ds(place, 128)].astype(jnp.float32)
                if number == masked and at < tap_count - 1:
                    value = value * keep_ref[0]
                for s in range(max(0, at - tap_count + 1), min(count, at + 1)):
                    term = value * taps[at - s]
                    totals[s] = term if totals[s] is None else totals[s] + term
                s = at - tap_count + 1
                if s >= 0:
                    joined[q, pl.ds((base + s) * inputs + h * half, half), pl.ds(lane, 128)] = totals[s].astype(
                        jnp.bfloat16
                    )
            base += count

    for at in range(len(groups)):
        for copy in copies(at):
            copy.start()
    for at, (q, h) in enumerate(groups):
        for copy in copies(at):
            copy.wait()
        if at == 0:
            for i in range(table_sems.shape[0]):
                table_copy(i).start()

        def columns(step, carry, q=q, h=h):
            filtered(q, h, step)
            return carry

        lax.fori_loop(0, channels // 128, columns, 0, unroll=2)
    for i in range(table_sems.shape[0]):
        table_copy(i).wait()
    count = table_ref.shape[0] // 2
    used = count - 16
    low = lax.broadcasted_iota(jnp.int32, (used // 8, 8, SIDE), 1)
    first, upper = low % 4 == 0, low < 4

    def product(table, q, side):
        return lax.dot_general(
            table_ref[pl.ds(table * count, count), :],
            joined[q, side, :],
            NT,
            preferred_element_type=jnp.float32,
        ).reshape(count // 8, 8, SIDE)

    def swapped(value):
        return jnp.concatenate([value[:, 4:], value[:, :4]], 1)

    sent = []
    for i in range(joined.shape[1] // SIDE):
        side = pl.ds(i * SIDE, SIDE)
        cosines = [product(0, q, side) for q in range(2)]
        sines = [product(1, q, side) for q in range(2)]
        sums = [cosines[0] + sines[1], cosines[1] - sines[0]]
        mirrored = [cosines[0] - sines[1], cosines[1] + sines[0]]
        sums = [x[: used // 8] for x in sums]
        mirrored = [jnp.where(first, x[1 : used // 8 + 1], x[: used // 8]) for x in mirrored]
        at = 0
        for real, imag in (sums, mirrored):
            for piece in (
                jnp.where(upper, real, swapped(imag)),
                jnp.where(upper, swapped(real), imag),
            ):
                out[pl.ds(at, used), side] = piece.reshape(used, SIDE).astype(jnp.bfloat16)
                at += used
        sent.append(pltpu.make_async_copy(out.at[:, side], out_hbm.at[:, side], out_sems.at[i]))
        sent[-1].start()
    for copy in sent:
        copy.wait()


SIDE = 256


def front(keep, operands, taps, table, segments, masked):
    inputs = operands[0].shape[1]
    channels = taps.shape[1]
    n_in = len(operands)
    cuts, bounds = strips(segments, n_in)
    size = 2 * channels
    lanes = inputs * sum(len(window) - taps.shape[0] + 1 for window in segments)
    return pl.pallas_call(
        functools.partial(front_kernel, inputs, channels, segments, masked, n_in),
        out_shape=jax.ShapeDtypeStruct((size, lanes), jnp.bfloat16),
        in_specs=[pl.BlockSpec(memory_space=pltpu.SMEM)]
        + [pl.BlockSpec(memory_space=pl.ANY)] * n_in
        + [pl.BlockSpec(memory_space=pltpu.VMEM), pl.BlockSpec(memory_space=pl.ANY)],
        out_specs=pl.BlockSpec(memory_space=pl.ANY),
        scratch_shapes=[pltpu.VMEM((2, inputs, span * channels), jnp.bfloat16) for _, span in bounds]
        + [
            pltpu.VMEM(table.shape, jnp.bfloat16),
            pltpu.VMEM((2, lanes, channels), jnp.bfloat16),
            pltpu.VMEM((size, lanes), jnp.bfloat16),
            pltpu.SemaphoreType.DMA((2 * (inputs // 16), len(cuts))),
            pltpu.SemaphoreType.DMA((2,)),
            pltpu.SemaphoreType.DMA((lanes // SIDE,)),
        ],
        compiler_params=pltpu.CompilerParams(vmem_limit_bytes=62 * 2**20),
        cost_estimate=pl.CostEstimate(
            flops=size * size * lanes, bytes_accessed=16 * 2**20, transcendentals=0
        ),
        name="front",
    )(keep, *operands, taps, table)


def sort_rows(times, parts):
    size = times * parts
    matrix = np.zeros((2, size, size), np.float32)
    for part in range(parts):
        for time in range(times):
            matrix[0, part * times + time, time * parts + part] = 1
            matrix[1, part * times + time, (times - 1 - time) * parts + part] = 1
    return matrix.astype(jnp.bfloat16)


def sort_lanes(group, block):
    size = group * group * block
    index = np.arange(size).reshape(group, group, block)
    matrix = np.zeros((size, size), np.float32)
    matrix[index.transpose(1, 0, 2).reshape(-1), np.arange(size)] = 1
    return matrix.astype(jnp.bfloat16)


def dot(left, right):
    return jnp.dot(left, right, preferred_element_type=jnp.float32).astype(jnp.bfloat16)


def dot_nt(left, right):
    return lax.dot_general(left, right, NT, preferred_element_type=jnp.float32).astype(jnp.bfloat16)


def gather_kernel(n_chan, got, rows_ref, lanes_ref, place_ref, out, sorted_rows, ordered):
    parts, times, total = ordered.shape
    block = got.shape[0] // n_chan
    n_time = block // parts
    frames = times // n_time
    group = 128 // (total // n_chan)
    for c in range(n_chan):
        at = pl.ds(c * block, block)
        sorted_rows[at, :] = dot(rows_ref[c // (n_chan // 2)], got[at, :])
    for a in range(n_chan // group):
        for g in range(frames // group):
            side = jnp.concatenate(
                [
                    sorted_rows[pl.ds((a * group + b) * block, block), pl.ds(g * 128, 128)]
                    for b in range(group)
                ],
                1,
            )
            turned = dot(side, lanes_ref[...])
            for j in range(group):
                for part in range(parts):
                    ordered[part, pl.ds((g * group + j) * n_time, n_time), pl.ds(a * 128, 128)] = turned[
                        part * n_time : (part + 1) * n_time, j * 128 : (j + 1) * 128
                    ]
    for part in range(parts):
        out[part // out.shape[1], part % out.shape[1]] = dot_nt(place_ref[...], ordered[part])


def gather(got, rows, lanes, place, n_chan, n_time, parts, limit):
    total = place.shape[0]
    times = n_time * got.shape[1] // (total // n_chan)
    return pl.pallas_call(
        functools.partial(gather_kernel, n_chan),
        out_shape=jax.ShapeDtypeStruct((2, parts // 2, total, times), jnp.bfloat16),
        in_specs=[pl.BlockSpec(memory_space=pltpu.VMEM)] * 4,
        out_specs=pl.BlockSpec(memory_space=pltpu.VMEM),
        scratch_shapes=[
            pltpu.VMEM(got.shape, jnp.bfloat16),
            pltpu.VMEM((parts, times, total), jnp.bfloat16),
        ],
        compiler_params=pltpu.CompilerParams(vmem_limit_bytes=limit),
        cost_estimate=pl.CostEstimate(flops=4 * 10**9, bytes_accessed=8 * 2**20, transcendentals=0),
        name="gather",
    )(got, rows, lanes, place)


LIMIT = 20 * 2**20
LIMIT_A = 56 * 2**20
LIMIT_B = 20 * 2**20


def correlate_kernel(scale, scalars, *refs):
    pieces, out = refs[:-1], refs[-1]
    for b in range(out.shape[1]):
        sides = []
        for end in range(2):
            at = pl.ds(pl.multiple_of(scalars[2 * b + end] * TILE, TILE), TILE)
            sides.append([jnp.concatenate([piece[0, 0, at, :], piece[1, 0, at, :]], 0) for piece in pieces])
        gram = sum(
            lax.dot_general(left, right, NT, preferred_element_type=jnp.float32)
            for left, right in zip(*sides)
        )
        out[0, b, 0] = (gram[:TILE, :TILE] + gram[TILE:, TILE:]) * scale
        out[0, b, 1] = (gram[TILE:, :TILE] - gram[:TILE, TILE:]) * scale


def correlate(pieces, pair_blocks, upper, scale):
    per_owner = pieces[0].shape[1]
    blocks = pair_blocks.shape[0]
    scalars = jnp.concatenate([pair_blocks.reshape(-1), upper.astype(jnp.int32).reshape(1)])

    def channel_of(j, scalars):
        return jnp.where(scalars[2 * blocks] > 0, lax.rem(per_owner - j, per_owner), j)

    return pl.pallas_call(
        functools.partial(correlate_kernel, scale),
        out_shape=jax.ShapeDtypeStruct((per_owner, blocks, 2, TILE, TILE), jnp.float32),
        grid_spec=pltpu.PrefetchScalarGridSpec(
            num_scalar_prefetch=1,
            grid=(per_owner,),
            in_specs=[pl.BlockSpec((2, 1) + x.shape[2:], lambda j, scalars: (0, j, 0, 0)) for x in pieces],
            out_specs=pl.BlockSpec(
                (1, blocks, 2, TILE, TILE), lambda j, scalars: (channel_of(j, scalars), 0, 0, 0, 0)
            ),
        ),
        compiler_params=pltpu.CompilerParams(vmem_limit_bytes=LIMIT),
        name="correlate",
    )(scalars, *pieces)


def local(voltages, filter_taps, slot_station, pair_blocks):
    tap_count, channels = filter_taps.shape
    inputs = voltages.shape[1]
    frame_count = voltages.shape[2] // channels
    n_chan = lax.axis_size("chan")
    n_time = lax.axis_size("tm")
    owners = n_chan * n_time
    per_owner = channels // owners
    parts = 2 * per_owner
    history = tap_count - 1
    ahead = history // 2
    cut = frame_count // 2
    table = jnp.asarray(dft_half(channels, per_owner))
    t = lax.axis_index("tm")
    keep = (t < n_time - 1).astype(jnp.float32).reshape(1)

    ranks = list(range(owners // 2)) + list(range(owners - 1, owners // 2 - 1, -1))

    def turn(spectra):
        pieces = spectra.reshape(owners, parts, -1)
        got = lax.all_to_all(
            pieces, OWNERS, split_axis=0, concat_axis=0, tiled=True, axis_index_groups=[ranks]
        )
        return got.reshape(owners * parts, -1)

    late = [[(0, f) for f in range(cut - history, frame_count)]]
    sent_late = front(keep, [voltages], filter_taps, table, late, None)
    got_late = turn(sent_late)
    behind = history - ahead
    tail = voltages[:, :, (frame_count - behind) * channels :]
    head = voltages[:, :, : ahead * channels]
    before = lax.ppermute(tail, "tm", [(i, i + 1) for i in range(n_time - 1)])
    after = lax.ppermute(head, "tm", [(i, (i - 1) % n_time) for i in range(n_time)])
    operands, _ = lax.optimization_barrier(([before, voltages, after], sent_late))
    early = [
        [(0, f) for f in range(behind)] + [(1, f) for f in range(cut)],
        [(1, f) for f in range(frame_count - history, frame_count)] + [(2, f) for f in range(ahead)],
    ]
    got_early = turn(front(keep, operands, filter_taps, table, early, 1))

    total = n_chan * inputs
    index = jnp.arange(total, dtype=jnp.int32)
    by_chan = slot_station.reshape(n_chan, -1)
    arrived = jnp.concatenate([by_chan[: n_chan // 2], by_chan[n_chan // 2 :][::-1]]).reshape(-1)
    station_in = jnp.repeat(arrived, 2)
    place = (station_in[None, :] == index[:, None] // 2) & (index[None, :] % 2 == index[:, None] % 2)
    place = place.astype(jnp.bfloat16)
    rows = jnp.asarray(sort_rows(n_time, parts))
    lanes = jnp.asarray(sort_lanes(128 // inputs, inputs))
    pieces = [
        gather(got, rows, lanes, place, n_chan, n_time, parts, limit)
        for got, limit in ((got_late, LIMIT_A), (got_early, LIMIT_B))
    ]
    upper = lax.axis_index("chan") >= n_chan // 2
    return correlate(pieces, pair_blocks, upper, 1.0 / (n_time * frame_count))


def solution(mesh):
    in_specs = (P(None, "chan", "tm"), P(), P(), P())
    out_specs = P(("chan", "tm"), None, None, None, None)
    return jax.shard_map(local, mesh=mesh, in_specs=in_specs, out_specs=out_specs, check_vma=False)
```

```python
import functools
import math

import jax
import jax.numpy as jnp
import numpy as np
from jax import lax
from jax.experimental import pallas as pl
from jax.experimental.pallas import tpu as pltpu
from jax.sharding import PartitionSpec as P

TILE = 128
OWNERS = ("chan", "tm")
NT = (((1,), (1,)), ((), ()))


def dft_half(channels, per_owner):
    index = np.arange(channels, dtype=np.int32)
    angles = (index[:, None] * index[None, :] % channels).astype(np.float32)
    angles = angles * np.float32(2.0 * math.pi / channels)
    half = channels // 2
    tiles = np.arange(half).reshape(2, -1, per_owner).transpose(1, 0, 2).reshape(-1)
    last = np.zeros(16, np.int32)
    last[0], last[per_owner] = half // 2, half
    picked = np.concatenate([tiles, last])
    tables = [f(angles[picked]) / np.float32(math.sqrt(channels)) for f in (np.cos, np.sin)]
    return np.concatenate(tables, 0).astype(jnp.bfloat16)


STRIP = 8


def strips(segments, n_in):
    cuts, bounds = [], []
    for operand in range(n_in):
        used = [at for window in segments for where, at in window if where == operand]
        first, last = min(used), max(used) + 1
        bounds.append((first, last - first))
        for start in range(first, last, STRIP):
            cuts.append((operand, start, min(STRIP, last - start)))
    return cuts, bounds


def front_kernel(inputs, channels, segments, masked, n_in, *refs):
    keep_ref, hbm = refs[0], refs[1 : 1 + n_in]
    taps_ref, table_hbm, out_hbm = refs[1 + n_in : 4 + n_in]
    bufs = refs[4 + n_in : 4 + 2 * n_in]
    table_ref, joined, out, sems, table_sems, out_sems = refs[4 + 2 * n_in :]
    tap_count = taps_ref.shape[0]
    half = 16
    groups = [(q, h) for q in range(2) for h in range(inputs // half)]
    cuts, bounds = strips(segments, n_in)

    def copies(at):
        q, h = groups[at]
        rows = pl.ds(h * half, half)
        return [
            pltpu.make_async_copy(
                hbm[p].at[q, rows, pl.ds(first * channels, count * channels)],
                bufs[p].at[q, rows, pl.ds((first - bounds[p][0]) * channels, count * channels)],
                sems.at[at, i],
            )
            for i, (p, first, count) in enumerate(cuts)
        ]

    def table_copy(i):
        size = table_ref.shape[0] // table_sems.shape[0]
        at = pl.ds(i * size, size)
        return pltpu.make_async_copy(table_hbm.at[at], table_ref.at[at], table_sems.at[i])

    def filtered(q, h, step):
        lane = pl.multiple_of(step * 128, 128)
        rows = pl.ds(h * half, half)
        taps = [taps_ref[pl.ds(t, 1), pl.ds(lane, 128)] for t in range(tap_count)]
        base = 0
        for number, window in enumerate(segments):
            count = len(window) - tap_count + 1
            totals = [None] * count
            for at, (operand, frame) in enumerate(window):
                place = pl.multiple_of((frame - bounds[operand][0]) * channels + lane, 128)
                value = bufs[operand][q, rows, pl.ds(place, 128)].astype(jnp.float32)
                if number == masked and at < tap_count - 1:
                    value = value * keep_ref[0]
                for s in range(max(0, at - tap_count + 1), min(count, at + 1)):
                    term = value * taps[at - s]
                    totals[s] = term if totals[s] is None else totals[s] + term
                s = at - tap_count + 1
                if s >= 0:
                    joined[q, pl.ds((base + s) * inputs + h * half, half), pl.ds(lane, 128)] = totals[s].astype(
                        jnp.bfloat16
                    )
            base += count

    for at in range(len(groups)):
        for copy in copies(at):
            copy.start()
    for at, (q, h) in enumerate(groups):
        for copy in copies(at):
            copy.wait()
        if at == 0:
            for i in range(table_sems.shape[0]):
                table_copy(i).start()

        def columns(step, carry, q=q, h=h):
            filtered(q, h, step)
            return carry

        lax.fori_loop(0, channels // 128, columns, 0, unroll=2)
    for i in range(table_sems.shape[0]):
        table_copy(i).wait()
    count = table_ref.shape[0] // 2
    used = count - 16
    low = lax.broadcasted_iota(jnp.int32, (used // 8, 8, SIDE), 1)
    first, upper = low % 4 == 0, low < 4

    def product(table, q, side):
        return lax.dot_general(
            table_ref[pl.ds(table * count, count), :],
            joined[q, side, :],
            NT,
            preferred_element_type=jnp.float32,
        ).reshape(count // 8, 8, SIDE)

    def swapped(value):
        return jnp.concatenate([value[:, 4:], value[:, :4]], 1)

    sent = []
    for i in range(joined.shape[1] // SIDE):
        side = pl.ds(i * SIDE, SIDE)
        cosines = [product(0, q, side) for q in range(2)]
        sines = [product(1, q, side) for q in range(2)]
        sums = [cosines[0] + sines[1], cosines[1] - sines[0]]
        mirrored = [cosines[0] - sines[1], cosines[1] + sines[0]]
        sums = [x[: used // 8] for x in sums]
        mirrored = [jnp.where(first, x[1 : used // 8 + 1], x[: used // 8]) for x in mirrored]
        at = 0
        for real, imag in (sums, mirrored):
            for piece in (
                jnp.where(upper, real, swapped(imag)),
                jnp.where(upper, swapped(real), imag),
            ):
                out[pl.ds(at, used), side] = piece.reshape(used, SIDE).astype(jnp.bfloat16)
                at += used
        sent.append(pltpu.make_async_copy(out.at[:, side], out_hbm.at[:, side], out_sems.at[i]))
        sent[-1].start()
    for copy in sent:
        copy.wait()


SIDE = 256


def front(keep, operands, taps, table, segments, masked):
    inputs = operands[0].shape[1]
    channels = taps.shape[1]
    n_in = len(operands)
    cuts, bounds = strips(segments, n_in)
    size = 2 * channels
    lanes = inputs * sum(len(window) - taps.shape[0] + 1 for window in segments)
    return pl.pallas_call(
        functools.partial(front_kernel, inputs, channels, segments, masked, n_in),
        out_shape=jax.ShapeDtypeStruct((size, lanes), jnp.bfloat16),
        in_specs=[pl.BlockSpec(memory_space=pltpu.SMEM)]
        + [pl.BlockSpec(memory_space=pl.ANY)] * n_in
        + [pl.BlockSpec(memory_space=pltpu.VMEM), pl.BlockSpec(memory_space=pl.ANY)],
        out_specs=pl.BlockSpec(memory_space=pl.ANY),
        scratch_shapes=[pltpu.VMEM((2, inputs, span * channels), jnp.bfloat16) for _, span in bounds]
        + [
            pltpu.VMEM(table.shape, jnp.bfloat16),
            pltpu.VMEM((2, lanes, channels), jnp.bfloat16),
            pltpu.VMEM((size, lanes), jnp.bfloat16),
            pltpu.SemaphoreType.DMA((2 * (inputs // 16), len(cuts))),
            pltpu.SemaphoreType.DMA((2,)),
            pltpu.SemaphoreType.DMA((lanes // SIDE,)),
        ],
        compiler_params=pltpu.CompilerParams(vmem_limit_bytes=62 * 2**20),
        cost_estimate=pl.CostEstimate(
            flops=size * size * lanes, bytes_accessed=16 * 2**20, transcendentals=0
        ),
        name="front",
    )(keep, *operands, taps, table)


def sort_rows(times, parts):
    size = times * parts
    matrix = np.zeros((2, size, size), np.float32)
    for part in range(parts):
        for time in range(times):
            matrix[0, part * times + time, time * parts + part] = 1
            matrix[1, part * times + time, (times - 1 - time) * parts + part] = 1
    return matrix.astype(jnp.bfloat16)


def sort_lanes(group, block):
    size = group * group * block
    index = np.arange(size).reshape(group, group, block)
    matrix = np.zeros((size, size), np.float32)
    matrix[index.transpose(1, 0, 2).reshape(-1), np.arange(size)] = 1
    return matrix.astype(jnp.bfloat16)


def dot(left, right):
    return jnp.dot(left, right, preferred_element_type=jnp.float32).astype(jnp.bfloat16)


def dot_nt(left, right):
    return lax.dot_general(left, right, NT, preferred_element_type=jnp.float32).astype(jnp.bfloat16)


def gather_kernel(n_chan, got, rows_ref, lanes_ref, place_ref, out, sorted_rows, ordered):
    parts, times, total = ordered.shape
    block = got.shape[0] // n_chan
    n_time = block // parts
    frames = times // n_time
    group = 128 // (total // n_chan)
    for c in range(n_chan):
        at = pl.ds(c * block, block)
        sorted_rows[at, :] = dot(rows_ref[c // (n_chan // 2)], got[at, :])
    for a in range(n_chan // group):
        for g in range(frames // group):
            side = jnp.concatenate(
                [
                    sorted_rows[pl.ds((a * group + b) * block, block), pl.ds(g * 128, 128)]
                    for b in range(group)
                ],
                1,
            )
            turned = dot(side, lanes_ref[...])
            for j in range(group):
                for part in range(parts):
                    ordered[part, pl.ds((g * group + j) * n_time, n_time), pl.ds(a * 128, 128)] = turned[
                        part * n_time : (part + 1) * n_time, j * 128 : (j + 1) * 128
                    ]
    for part in range(parts):
        out[part // out.shape[1], part % out.shape[1]] = dot_nt(place_ref[...], ordered[part])


def gather(got, rows, lanes, place, n_chan, n_time, parts, limit):
    total = place.shape[0]
    times = n_time * got.shape[1] // (total // n_chan)
    return pl.pallas_call(
        functools.partial(gather_kernel, n_chan),
        out_shape=jax.ShapeDtypeStruct((2, parts // 2, total, times), jnp.bfloat16),
        in_specs=[pl.BlockSpec(memory_space=pltpu.VMEM)] * 4,
        out_specs=pl.BlockSpec(memory_space=pltpu.VMEM),
        scratch_shapes=[
            pltpu.VMEM(got.shape, jnp.bfloat16),
            pltpu.VMEM((parts, times, total), jnp.bfloat16),
        ],
        compiler_params=pltpu.CompilerParams(vmem_limit_bytes=limit),
        cost_estimate=pl.CostEstimate(flops=4 * 10**9, bytes_accessed=8 * 2**20, transcendentals=0),
        name="gather",
    )(got, rows, lanes, place)


LIMIT = 20 * 2**20
LIMIT_A = 56 * 2**20
LIMIT_B = 20 * 2**20


def correlate_kernel(first, scale, scalars, piece, *refs):
    partial, (out_hbm, out, sems) = refs[0], refs[-3:]
    per_owner, blocks = out.shape[:2]

    def send(j):
        channel = j
        if not first:
            channel = jnp.where(scalars[2 * blocks] > 0, (per_owner - j) % per_owner, j)
        return pltpu.make_async_copy(out.at[j], out_hbm.at[channel], sems.at[j])

    for j in range(per_owner):
        for b in range(blocks):
            sides = []
            for end in range(2):
                at = pl.ds(pl.multiple_of(scalars[2 * b + end] * TILE, TILE), TILE)
                sides.append(jnp.concatenate([piece[0, j, at, :], piece[1, j, at, :]], 0))
            gram = lax.dot_general(*sides, NT, preferred_element_type=jnp.float32)
            real = gram[:TILE, :TILE] + gram[TILE:, TILE:]
            imag = gram[TILE:, :TILE] - gram[:TILE, TILE:]
            if first:
                out[j, b, 0], out[j, b, 1] = real, imag
            else:
                out[j, b, 0] = (real + partial[j, b, 0]) * scale
                out[j, b, 1] = (imag + partial[j, b, 1]) * scale
        send(j).start()
    for j in range(per_owner):
        send(j).wait()


def correlate(piece, partial, pair_blocks, upper, scale):
    per_owner = piece.shape[1]
    blocks = pair_blocks.shape[0]
    scalars = jnp.concatenate([pair_blocks.reshape(-1), upper.astype(jnp.int32).reshape(1)])
    shape = (per_owner, blocks, 2, TILE, TILE)
    first = partial is None
    operands = [piece] if first else [piece, partial]
    return pl.pallas_call(
        functools.partial(correlate_kernel, first, scale),
        out_shape=jax.ShapeDtypeStruct(shape, jnp.float32),
        in_specs=[pl.BlockSpec(memory_space=pltpu.SMEM)] + [pl.BlockSpec(memory_space=pltpu.VMEM)] * len(operands),
        out_specs=pl.BlockSpec(memory_space=pl.ANY),
        scratch_shapes=[pltpu.VMEM(shape, jnp.float32), pltpu.SemaphoreType.DMA((per_owner,))],
        compiler_params=pltpu.CompilerParams(vmem_limit_bytes=LIMIT),
        cost_estimate=pl.CostEstimate(flops=3 * 10**9, bytes_accessed=8 * 2**20, transcendentals=0),
        name="correlate",
    )(scalars, *operands)


def local(voltages, filter_taps, slot_station, pair_blocks):
    tap_count, channels = filter_taps.shape
    inputs = voltages.shape[1]
    frame_count = voltages.shape[2] // channels
    n_chan = lax.axis_size("chan")
    n_time = lax.axis_size("tm")
    owners = n_chan * n_time
    per_owner = channels // owners
    parts = 2 * per_owner
    history = tap_count - 1
    ahead = history // 2
    cut = frame_count // 2
    table = jnp.asarray(dft_half(channels, per_owner))
    t = lax.axis_index("tm")
    keep = (t < n_time - 1).astype(jnp.float32).reshape(1)

    ranks = list(range(owners // 2)) + list(range(owners - 1, owners // 2 - 1, -1))

    def turn(spectra):
        pieces = spectra.reshape(owners, parts, -1)
        got = lax.all_to_all(
            pieces, OWNERS, split_axis=0, concat_axis=0, tiled=True, axis_index_groups=[ranks]
        )
        return got.reshape(owners * parts, -1)

    late = [[(0, f) for f in range(cut - history, frame_count)]]
    sent_late = front(keep, [voltages], filter_taps, table, late, None)
    got_late = turn(sent_late)
    behind = history - ahead
    tail = voltages[:, :, (frame_count - behind) * channels :]
    head = voltages[:, :, : ahead * channels]
    before = lax.ppermute(tail, "tm", [(i, i + 1) for i in range(n_time - 1)])
    after = lax.ppermute(head, "tm", [(i, (i - 1) % n_time) for i in range(n_time)])
    operands, _ = lax.optimization_barrier(([before, voltages, after], sent_late))
    early = [
        [(0, f) for f in range(behind)] + [(1, f) for f in range(cut)],
        [(1, f) for f in range(frame_count - history, frame_count)] + [(2, f) for f in range(ahead)],
    ]
    got_early = turn(front(keep, operands, filter_taps, table, early, 1))

    total = n_chan * inputs
    index = jnp.arange(total, dtype=jnp.int32)
    by_chan = slot_station.reshape(n_chan, -1)
    arrived = jnp.concatenate([by_chan[: n_chan // 2], by_chan[n_chan // 2 :][::-1]]).reshape(-1)
    station_in = jnp.repeat(arrived, 2)
    place = (station_in[None, :] == index[:, None] // 2) & (index[None, :] % 2 == index[:, None] % 2)
    place = place.astype(jnp.bfloat16)
    rows = jnp.asarray(sort_rows(n_time, parts))
    lanes = jnp.asarray(sort_lanes(128 // inputs, inputs))
    upper = lax.axis_index("chan") >= n_chan // 2
    scale = 1.0 / (n_time * frame_count)
    result = None
    for got, limit in ((got_late, LIMIT_A), (got_early, LIMIT_B)):
        piece = gather(got, rows, lanes, place, n_chan, n_time, parts, limit)
        result = correlate(piece, result, pair_blocks, upper, scale)
    return result


def solution(mesh):
    in_specs = (P(None, "chan", "tm"), P(), P(), P())
    out_specs = P(("chan", "tm"), None, None, None, None)
    return jax.shard_map(local, mesh=mesh, in_specs=in_specs, out_specs=out_specs, check_vma=False)
```
